32 devices in a mesh: grp: 4 (over y, core), lon: 4 (over z), lat: 2 (over x).
Axes of the slice: x: 2, y: 2, z: 4, core: 2. Of those that a mesh axis runs over, the one named last changes fastest.
Arguments:
- state: float32 [4, 40, 96, 256], P('grp', None, 'lon', 'lat'), may hold values from -6 to 6
- depth: int32 [96, 256], P('lon', 'lat'), may hold values from 0 to 6
- rates: float32 [20, 20], replicated, may hold values from -1.25 to 1.25
- grazing: float32 [20], replicated, may hold values from -3 to 3
Outputs:
- state_out: float32 [4, 40, 96, 256], P('grp', None, 'lon', 'lat')
The draws below stay inside these ranges and needn't reach their ends.
Inputs may be any that keep to these rules, and one draw needn't show every extreme that they name: `depth`: number of wet levels of a column; 0 is land.
All inputs are finite; a program needn't handle non-finite values.
Results may differ from the reference program's by a relative error of at most 0.0003.
Values sent between devices are 32-bit elements; how exact they have to be, the bound alone decides.
A program may use at most 64 MiB of HBM per device.

```python
import jax
import jax.numpy as jnp
from jax import lax

LZ = 2
NTR = 20
SECTIONS = 4
NSUB = 4
NZ = 6
NX = 96
NY = 256
NF = 40
N_GRP = 4


def with_ends(array, stream_key, least, largest):
    longest = array.shape.index(max(array.shape))
    spots = []
    for shift in (0, 1):
        where = [jax.random.randint(jax.random.fold_in(stream_key, axis), (), 0, length) for axis, length in enumerate(array.shape)]
        where[longest] = (where[longest] + shift) % array.shape[longest]
        spots.append(tuple(where))
    return array.at[spots[0]].set(least).at[spots[1]].set(largest)


def levels(own_key, extent, shards, smallest, largest):
    level, own = 1.0, jax.random.fold_in(own_key, 6)
    for dim, parts in shards:
        heights = jnp.exp(jax.random.uniform(jax.random.fold_in(own, dim), (parts,), jnp.float32, smallest / len(shards), largest / len(shards)))
        level = level * jnp.repeat(heights, extent[dim] // parts).reshape([-1 if axis == dim else 1 for axis in range(len(extent))])
    return level


def noise(own_key, dims, width, bound, split=(), kind=jnp.bfloat16):
    level = levels(own_key, dims, split, -0.22, 0.18) if split else 1.0
    values = jax.random.normal(own_key, dims, jnp.float32) * width * level
    return jnp.minimum(jnp.maximum(values, -bound), bound).astype(kind)


def setup_inputs(seed: int = 0) -> dict:
    seeds = jax.random.split(jax.random.key(seed), 5)
    return {
        "state": noise(seeds[0], (N_GRP, NF, NX, NY), 1.0, 6.0, ((0, 4), (2, 4), (3, 2)), jnp.float32),
        "depth": with_ends(jax.random.randint(seeds[1], (NX, NY), 0, NZ + 1), jax.random.fold_in(seeds[1], 1), 0, NZ).astype(jnp.int32),
        "rates": noise(seeds[2], (NTR, NTR), NTR ** -0.5, 1.25, (), jnp.float32),
        "grazing": noise(seeds[3], (NTR,), 0.5, 3.0, (), jnp.float32),
    }


def pad_grid(field):
    field = jnp.concatenate([field[..., -1:, :], field, field[..., :1, :]], axis=-2)
    zeros_rim = jnp.zeros(field.shape[:-1] + (1,), field.dtype)
    return jnp.concatenate([zeros_rim, field, zeros_rim], axis=-1)


def center_of(padded):
    return padded[..., 1:-1, 1:-1]


def grad_x(padded):
    return padded[..., 2:, 1:-1] - padded[..., :-2, 1:-1]


def grad_y(padded):
    return padded[..., 1:-1, 2:] - padded[..., 1:-1, :-2]


def laplace(padded):
    return padded[..., 2:, 1:-1] + padded[..., :-2, 1:-1] + padded[..., 1:-1, 2:] + padded[..., 1:-1, :-2] - 4.0 * center_of(padded)


def advance_dynamics(zonal_pad, merid_pad, temp_pad, surf_pad, wet_mask, land_mask, coriolis_rows):
    zonal = center_of(zonal_pad)
    merid = center_of(merid_pad)
    temper = center_of(temp_pad)
    surface = center_of(surf_pad)
    divergence = jnp.sum(grad_x(zonal_pad) + grad_y(merid_pad), axis=0)
    zonal_new = wet_mask * (zonal + coriolis_rows * merid - 0.5 * grad_x(surf_pad))
    merid_new = wet_mask * (merid - coriolis_rows * zonal - 0.5 * grad_y(surf_pad))
    surface_new = land_mask * (surface - (0.25 / zonal.shape[0]) * divergence)
    temper_new = wet_mask * (temper - 0.25 * (zonal * grad_x(temp_pad) + merid * grad_y(temp_pad)) + 0.1 * laplace(temp_pad))
    return zonal_new, merid_new, temper_new, surface_new


def advect_tracers(tracer_pad, zonal, merid, wet_mask):
    return wet_mask * (center_of(tracer_pad) - 0.25 * (zonal * grad_x(tracer_pad) + merid * grad_y(tracer_pad)) + 0.1 * laplace(tracer_pad))


def reference(state, depth, rates, grazing):
    groups = N_GRP
    level_index = jnp.arange(NZ, dtype=jnp.int32)[:, None, None]
    wet_mask = (level_index < depth[None]).astype(state.dtype)
    land_mask = (depth > 0).astype(state.dtype)
    lat_coord = jnp.arange(NY).astype(state.dtype)
    coriolis_rows = 0.3 * jnp.sin(jnp.pi * (lat_coord + 0.5) / NY - jnp.pi / 2)
    dynamic = state[0]
    zonal = dynamic[:NZ]
    merid = dynamic[NZ:2 * NZ]
    temper = dynamic[2 * NZ:3 * NZ]
    surface = dynamic[3 * NZ]
    for section_index in range(SECTIONS):
        zonal, merid, temper, surface = advance_dynamics(pad_grid(zonal), pad_grid(merid), pad_grid(temper), pad_grid(surface), wet_mask, land_mask, coriolis_rows)
    tracers = state[1:].reshape(groups - 1, NTR, LZ, NX, NY)
    tracers = jnp.transpose(tracers, (1, 0, 2, 3, 4)).reshape(NTR, NZ, NX, NY)

    def transport(single):
        for sub_index in range(NSUB):
            single = advect_tracers(pad_grid(single), zonal, merid, wet_mask)
        return single

    tracers = lax.map(transport, tracers)
    kinetic = jnp.einsum('ts,szxy->tzxy', rates, tracers, precision=lax.Precision.HIGHEST)
    kinetic = kinetic + grazing[:, None, None, None] * (tracers[0] * tracers[1])[None]
    updated = wet_mask[None] * (tracers + 0.2 * jnp.exp(0.05 * temper)[None] * kinetic)
    light_factor = jnp.exp(-(level_index.astype(state.dtype) + 0.5) / NZ)
    heating = 0.3 * wet_mask * updated[0] * light_factor
    temper_final = temper + heating
    unused = jnp.zeros((NF - 3 * NZ - 1, NX, NY), state.dtype)
    first_slot = jnp.concatenate([zonal, merid, temper_final, surface[None], unused], axis=0)
    tracer_slots = updated.reshape(NTR, groups - 1, LZ, NX, NY)
    tracer_slots = jnp.transpose(tracer_slots, (1, 0, 2, 3, 4)).reshape(groups - 1, NF, NX, NY)
    return jnp.concatenate([first_slot[None], tracer_slots], axis=0)
```

```python
import functools

import jax
import jax.numpy as jnp
from jax import lax
from jax.experimental import pallas as pl
from jax.experimental.pallas import tpu as pltpu
from jax.sharding import PartitionSpec as P

LZ = 2
NTR = 20
SECTIONS = 4
NSUB = 4
HD = SECTIONS + NSUB - 1
HT = NSUB
HV = NSUB - 1
WD = HD + 11
MESH = pl.DeviceIdType.MESH
F32 = jnp.float32


def roll(a, shift, axis=None):
    axis = a.ndim - 1 if axis is None else axis
    shift = shift % a.shape[axis]
    return a if shift == 0 else pltpu.roll(a, shift, axis)


def each(count, step):
    def one(i, carry):
        step(i)
        return carry

    lax.fori_loop(0, count, one, 0, unroll=True)


def kernel(
    groups, lons, lats,
    state, depth, rates, grazing, out,
    dyn_a, dyn_b, wet_d, land_d, edge, low, high, pack_core, pack_strip,
    got_core, got_strip, tr_a, tr_b, st_a, st_b, coef, coef_s, extra, theta_send, theta_got,
    send_sem, recv_sem, pack_send, pack_recv, back_send, back_recv,
):
    nx, ny = depth.shape
    levels = LZ * (groups - 1)
    tiles = state.shape[0] // nx // 8
    member = lax.axis_index("grp")
    lon = lax.axis_index("lon")
    lat = lax.axis_index("lat")
    has_low = lat > 0
    has_high = lat < lats - 1
    lane = lax.broadcasted_iota(jnp.int32, (8, ny), 1)
    sub = lax.broadcasted_iota(jnp.int32, (8, ny), 0)
    half = lane % 64
    is_low = lane < 64

    def peer(dx, dy):
        return (member, (lon + dx + lons) % lons, lat + dy)

    barrier = pltpu.get_barrier_semaphore()

    def signal(device):
        pl.semaphore_signal(barrier, inc=1, device_id=device, device_id_type=MESH)

    for dx in (-1, 1):
        signal(peer(dx, 0))

    @pl.when(has_low)
    def _():
        for dx in (-1, 0, 1):
            signal(peer(dx, -1))

    @pl.when(has_high)
    def _():
        for dx in (-1, 0, 1):
            signal(peer(dx, 1))

    @pl.when(member == 0)
    def _():
        for m in range(1, groups):
            signal((m, lon, lat))

    @pl.when(member != 0)
    def _():
        signal((0, lon, lat))

    @pl.when(lat == 0)
    def _():
        low[...] = jnp.zeros(low.shape, F32)

    @pl.when(lat == lats - 1)
    def _():
        high[...] = jnp.zeros(high.shape, F32)

    def barrier_wait():
        beside = has_low.astype(jnp.int32) + has_high.astype(jnp.int32)
        pl.semaphore_wait(barrier, 2 + 3 * beside + jnp.where(member == 0, groups - 1, 1))

    def exchange(core, h):
        copies = []
        for dy in (0, -1, 1):
            for dx in (-1, 0, 1):
                if dx == 0 and dy == 0:
                    continue
                start = nx - h if dx == 1 else 0
                size = h if dx else nx
                to = {1: 0, 0: h, -1: h + nx}[dx]
                if dy == 0:
                    src = core(h + start, size)
                    dst = core(to, size)
                else:
                    src = edge.at[pl.ds(start, size)]
                    dst = (low if dy == 1 else high).at[pl.ds(to, size)]
                index = (dy + 1) * 3 + dx + 1
                copy = pltpu.make_async_remote_copy(
                    src_ref=src, dst_ref=dst,
                    send_sem=send_sem.at[index], recv_sem=recv_sem.at[index],
                    device_id=peer(dx, dy), device_id_type=MESH,
                )
                copies.append((dy, copy))

        def guarded(there, action):
            if there is None:
                action()
            else:
                pl.when(there)(action)

        sends = {0: None, -1: has_low, 1: has_high}
        comes = {0: None, -1: has_high, 1: has_low}

        def start():
            for dy, copy in copies:
                guarded(sends[dy], copy.start)

        def arrived():
            for dy, copy in copies:
                guarded(comes[dy], copy.wait_recv)

        def left():
            for dy, copy in copies:
                guarded(sends[dy], copy.wait_send)

        return start, arrived, left

    def pack_copies(m):
        pairs = ((pack_core, got_core), (pack_strip, got_strip))
        return [
            pltpu.make_async_remote_copy(
                src_ref=src.at[m - 1], dst_ref=dst,
                send_sem=pack_send.at[m - 1, i], recv_sem=pack_recv.at[i],
                device_id=(m, lon, lat), device_id_type=MESH,
            )
            for i, (src, dst) in enumerate(pairs)
        ]

    def back_copy(m):
        return pltpu.make_async_remote_copy(
            src_ref=theta_send, dst_ref=theta_got.at[m - 1],
            send_sem=back_send, recv_sem=back_recv.at[m - 1],
            device_id=(0, lon, lat), device_id_type=MESH,
        )

    @pl.when(member == 0)
    def _():
        def load(x):
            dep = jnp.broadcast_to(depth[pl.ds(x, 1), :].astype(F32), (8, ny))
            eta = jnp.broadcast_to(state[pl.ds(3 * levels * nx + x, 1), :], (8, ny))
            fields = [
                jnp.where(sub < levels, state[pl.ds(q * levels * nx + x, 8, stride=nx), :], 0.0)
                for q in range(3)
            ]
            fields.append(jnp.where(sub < 4, eta, dep))
            packet = jnp.zeros((8, ny), F32)
            for q in range(4):
                dyn_a[HD + x, 0, q] = fields[q]
                near = jnp.where(is_low, roll(fields[q], HD + HD * q), roll(fields[q], 75 + HD * q))
                begin = jnp.where(is_low, HD * q, 75 + HD * q)
                packet = jnp.where((lane >= begin) & (lane < begin + HD), near, packet)
            edge[x] = packet

        each(nx, load)
        start, arrived, left = exchange(lambda at, size: dyn_a.at[pl.ds(at, size), 0], HD)
        barrier_wait()
        start()
        arrived()
        left()

        level = sub.astype(F32)

        def unpack(r):
            from_low = low[r]
            from_high = high[r]
            for q in range(4):
                field = dyn_a[r, 0, q]
                strip = jnp.where(is_low, roll(field, HD), roll(field, 75))
                strip = jnp.where(lane < HD, roll(from_low, -HD * q), strip)
                strip = jnp.where((lane >= 75) & (lane < 75 + HD), roll(from_high, -HD * q), strip)
                if q < 3:
                    dyn_a[r, 1, q] = strip
                else:
                    for i, both in enumerate((field, strip)):
                        dyn_a[r, i, 3] = jnp.broadcast_to(both[0:1], (8, ny))
                        dep = jnp.broadcast_to(both[4:5], (8, ny))
                        wet_d[r, i] = (level < dep).astype(F32)
                        land_d[r, i] = dep

        each(nx + 2 * HD, unpack)

        def rows_of(lat_index):
            return 0.3 * jnp.sin(jnp.pi * (lat_index.astype(F32) + 0.5) / (lats * ny) - jnp.pi / 2)

        base = lat * ny
        strip_y = jnp.where(is_low, lane - HD, lane - 64 + ny - 11)
        cor = jnp.stack([rows_of(base + lane), rows_of(base + strip_y)])
        current, following = dyn_a, dyn_b
        for section in range(SECTIONS):
            def advance(i, section=section, current=current, following=following):
                r = i + section + 1
                u, v, th, eta = (current[r, :, q] for q in range(4))
                up, tp, ep = (current[r + 1, :, q] for q in (0, 2, 3))
                um, tm, em = (current[r - 1, :, q] for q in (0, 2, 3))
                vyp, vym = roll(v, -1), roll(v, 1)
                typ, tym = roll(th, -1), roll(th, 1)
                eyp, eym = roll(eta, -1), roll(eta, 1)
                wet = wet_d[r]
                div = jnp.sum((up - um) + (vyp - vym), axis=1, keepdims=True)
                new_eta = eta - (0.25 / levels) * div
                results = (
                    wet * (u + cor * v - 0.5 * (ep - em)),
                    wet * (v - cor * u - 0.5 * (eyp - eym)),
                    wet * (
                        th - 0.25 * (u * (tp - tm) + v * (typ - tym))
                        + 0.1 * (((tp + tm) + (typ + tym)) - 4.0 * th)
                    ),
                    jnp.where(land_d[r] > 0, new_eta, 0.0),
                )
                for q, new in enumerate(results):
                    if section < SECTIONS - 1:
                        following[r, :, q] = new
                    else:
                        core = jnp.where(lane < 4, roll(new[1], -HD), new[0])
                        core = jnp.where(lane >= ny - 4, roll(new[1], ny - 4 - 64 - HD), core)
                        following[r, 0, q] = core
                        following[r, 1, q] = new[1]

            each(nx + 2 * HD - 2 * (section + 1), advance)
            current, following = following, current

        def bundle(i):
            strips = [None] * (groups - 1)
            for part in range(3):
                r = SECTIONS + 3 * i + part
                u, v, th = (current[r, :, q] for q in range(3))
                dep = land_d[r]
                for m in range(groups - 1):
                    both = jnp.where(sub < 6, roll(th, 4 - LZ * m, 1), dep)
                    both = jnp.where(sub < 4, roll(v, 2 - LZ * m, 1), both)
                    both = jnp.where(sub < 2, roll(u, -LZ * m, 1), both)
                    pack_core[m, 3 * i + part] = both[0]
                    moved = roll(both[1], WD * part)
                    if part == 0:
                        strips[m] = moved
                    else:
                        strips[m] = jnp.where(half >= WD * part, moved, strips[m])
            for m in range(groups - 1):
                pack_strip[m, i] = strips[m]

        each((nx + 2 * HV) // 3, bundle)
        for m in range(1, groups):
            for copy in pack_copies(m):
                copy.start()

        def emit(x):
            for q in range(2):
                out[pl.ds(q * levels * nx + x, levels, stride=nx), :] = current[HD + x, 0, q][:levels]
            out[pl.ds(3 * levels * nx + x, 1), :] = current[HD + x, 0, 3][0:1]

        each(nx, emit)
        used = (3 * levels + 1) * nx
        out[used:, :] = jnp.zeros((out.shape[0] - used, ny), F32)
        for m in range(1, groups):
            for copy in pack_copies(m):
                copy.wait_send()
        for m in range(1, groups):
            back_copy(m).wait_recv()
        for m in range(1, groups):
            at = (2 * levels + LZ * (m - 1)) * nx
            out[at : at + LZ * nx, :] = theta_got[m - 1]

    @pl.when(member != 0)
    def _():
        place = half % 12
        slot = half // 12

        def load(x):
            near = jnp.zeros((8, ny), F32)
            for j in range(tiles):
                tile = state[pl.ds(8 * j * nx + x, 8, stride=nx), :]
                tr_a[HT + x, j] = tile
                moved = jnp.where(is_low, roll(tile, 12 * j + 4), roll(tile, 12 * j + 72))
                near = jnp.where(slot == j, moved, near)
            edge[x] = near

        each(nx, load)
        start, arrived, left = exchange(lambda at, size: tr_a.at[pl.ds(at, size)], HT)
        barrier_wait()
        start()

        rows = LZ * NTR
        spread = (
            lax.broadcasted_iota(jnp.int32, (rows, NTR), 0) // LZ
            == lax.broadcasted_iota(jnp.int32, (rows, NTR), 1)
        ).astype(F32)
        spread_t = (
            lax.broadcasted_iota(jnp.int32, (NTR, rows), 1) // LZ
            == lax.broadcasted_iota(jnp.int32, (NTR, rows), 0)
        ).astype(F32)
        exact = dict(precision=lax.Precision.HIGHEST, preferred_element_type=F32)
        wide = jnp.dot(jnp.dot(spread, rates[...], **exact), spread_t, **exact)
        same = (
            lax.broadcasted_iota(jnp.int32, (rows, rows), 0) % LZ
            == lax.broadcasted_iota(jnp.int32, (rows, rows), 1) % LZ
        )
        wide = jnp.where(same, wide, 0.0)
        wide_hi = wide.astype(jnp.bfloat16).astype(F32)
        wide_lo = wide - wide_hi
        mixing = jnp.concatenate([wide_hi, wide_hi, wide_lo], axis=1)
        graze = jnp.sum(spread * grazing[...], axis=1, keepdims=True)
        graze = jnp.broadcast_to(graze, (rows, ny)).reshape(tiles, 8, ny)

        arrived()
        left()

        def join(r):
            near = jnp.zeros((8, ny), F32)
            for j in range(tiles):
                tile = tr_a[r, j]
                moved = jnp.where(is_low, roll(tile, 12 * j + 4), roll(tile, 12 * j + 72))
                near = jnp.where(slot == j, moved, near)
            near = jnp.where(is_low & (place < 4), low[r], near)
            near = jnp.where((lane >= 64) & (place >= 8), high[r], near)
            st_a[r] = near

        each(nx + 2 * HT, join)

        first = LZ * (member - 1)
        odd = sub % LZ
        level = (first + odd).astype(F32)
        for copy in pack_copies(1):
            copy.wait_recv()

        def pattern(v, i):
            return jnp.where(odd == 0, v[i : i + 1], v[i + 1 : i + 2])

        def factors(packet, target, r):
            u = pattern(packet, 0)
            v = pattern(packet, 2)
            wet = (level < packet[6:7]).astype(F32)
            target[r, 0] = 0.6 * wet
            for i, value in enumerate((u, v)):
                target[r, 2 * i + 1] = wet * (0.1 - 0.25 * value)
                target[r, 2 * i + 2] = wet * (0.1 + 0.25 * value)
            return wet

        def coefficients(i):
            strip = got_strip[i]
            for part in range(3):
                r = 3 * i + part
                packet = got_core[r]
                wet = factors(packet, coef, r)
                extra[r, 0] = wet
                extra[r, 1] = pattern(packet, 4)
                spread_strip = roll(strip, -3 - WD * part)
                for j in range(1, tiles):
                    moved = roll(strip, 12 * j - 3 - WD * part)
                    spread_strip = jnp.where(slot == j, moved, spread_strip)
                factors(spread_strip, coef_s, r)

        each((nx + 2 * HV) // 3, coefficients)

        cur, nxt, cur_s, nxt_s = tr_a, tr_b, st_a, st_b
        for step in range(NSUB):
            def advance(i, step=step, cur=cur, nxt=nxt, cur_s=cur_s, nxt_s=nxt_s):
                r = i + step + 1
                a, xp, xm, yp, ym = (coef[r - 1, k] for k in range(5))
                for j in range(tiles):
                    c = cur[r, j]
                    nxt[r, j] = (a * c + (xp * cur[r + 1, j] + xm * cur[r - 1, j])) + (
                        yp * roll(c, -1) + ym * roll(c, 1)
                    )
                a, xp, xm, yp, ym = (coef_s[r - 1, k] for k in range(5))
                c = cur_s[r]
                nxt_s[r] = (a * c + (xp * cur_s[r + 1] + xm * cur_s[r - 1])) + (
                    yp * roll(c, -1) + ym * roll(c, 1)
                )

            each(nx + 2 * HT - 2 * (step + 1), advance)
            cur, nxt, cur_s, nxt_s = nxt, cur, nxt_s, cur_s

        light = 0.3 * jnp.exp(-(level + 0.5) / levels)

        def react(x):
            strip = cur_s[HT + x]
            parts = []
            for j in range(tiles):
                c = cur[HT + x, j]
                c = jnp.where(lane < 4, roll(strip, -12 * j - 4), c)
                parts.append(jnp.where(lane >= ny - 4, roll(strip, 56 - 12 * j), c))
            c = jnp.concatenate(parts, axis=0)
            c_hi = c.astype(jnp.bfloat16).astype(F32)
            stacked = jnp.concatenate([c_hi, c - c_hi, c_hi], axis=0)
            kinetic = jnp.dot(mixing, stacked, preferred_element_type=F32)
            product = parts[0] * roll(parts[0], -LZ, 0)
            product = pattern(product, 0)
            wet = extra[HV + x, 0]
            th = extra[HV + x, 1]
            growth = 0.2 * jnp.exp(0.05 * th)
            for j in range(tiles):
                both = kinetic[8 * j : 8 * j + 8] + graze[j] * product
                new = wet * (parts[j] + growth * both)
                out[pl.ds(8 * j * nx + x, 8, stride=nx), :] = new
                if j == 0:
                    final = th + light * wet * new
                    theta_send[pl.ds(x, LZ, stride=nx), :] = final[:LZ]

        each(nx, react)
        back = back_copy(member)
        back.start()
        back.wait_send()


def solution(mesh):
    groups, lons, lats = (mesh.shape[a] for a in ("grp", "lon", "lat"))

    def body(state, depth, rates, grazing):
        _, planes, nx, ny = state.shape
        tiles = planes // 8
        xd, xt, xv = nx + 2 * HD, nx + 2 * HT, nx + 2 * HV
        vmem = lambda *shape: pltpu.VMEM(shape, F32)
        dma = pltpu.SemaphoreType.DMA
        flat = pl.pallas_call(
            functools.partial(kernel, groups, lons, lats),
            out_shape=jax.ShapeDtypeStruct((planes * nx, ny), F32),
            in_specs=[pl.BlockSpec(memory_space=pltpu.VMEM)] * 4,
            out_specs=pl.BlockSpec(memory_space=pltpu.VMEM),
            scratch_shapes=[
                vmem(xd, 2, 4, 8, ny), vmem(xd, 2, 4, 8, ny),
                vmem(xd, 2, 8, ny), vmem(xd, 2, 8, ny),
                vmem(nx, 8, ny), vmem(xd, 8, ny), vmem(xd, 8, ny),
                vmem(groups - 1, xv, 8, ny), vmem(groups - 1, xv // 3, 8, ny),
                vmem(xv, 8, ny), vmem(xv // 3, 8, ny),
                vmem(xt, tiles, 8, ny), vmem(xt, tiles, 8, ny),
                vmem(xt, 8, ny), vmem(xt, 8, ny),
                vmem(xv, 5, 8, ny), vmem(xv, 5, 8, ny), vmem(xv, 2, 8, ny),
                vmem(LZ * nx, ny), vmem(groups - 1, LZ * nx, ny),
                dma((9,)), dma((9,)), dma((groups - 1, 2)), dma((2,)), dma, dma((groups - 1,)),
            ],
            compiler_params=pltpu.CompilerParams(
                collective_id=0, has_side_effects=True, vmem_limit_bytes=40 * 2**20
            ),
            cost_estimate=pl.CostEstimate(
                flops=40_000_000, bytes_accessed=8 * planes * nx * ny, transcendentals=8192
            ),
        )(state.reshape(planes * nx, ny), depth, rates, grazing.reshape(1, NTR))
        return flat.reshape(state.shape)

    return jax.shard_map(
        body, mesh=mesh,
        in_specs=(P("grp", None, "lon", "lat"), P("lon", "lat"), P(), P()),
        out_specs=P("grp", None, "lon", "lat"), check_vma=False,
    )
```
